32 devices in a mesh: grp: 2 (over y), sec: 4 (over z), term: 4 (over x, core).
Axes of the slice: x: 2, y: 2, z: 4, core: 2. Of those that a mesh axis runs over, the one named last changes fastest.
Arguments:
- wave_blocks: bfloat16 [16, 16, 128, 128], P(('grp', 'sec')), parts along dimension 0, may hold values from -6 to 6
- right_env: bfloat16 [48, 8, 128, 128], P(('grp', 'term'), 'sec'), parts along dimension 0, may hold values from -0.5 to 0.5
- left_env: bfloat16 [48, 8, 128, 128], P(('grp', 'term'), 'sec'), parts along dimension 0, may hold values from -0.5 to 0.5
- site_coeff: float32 [48, 16], P(('grp', 'term')), parts along dimension 0, may hold values from -0.4 to 0.4
- dest_owner: int32 [16, 16, 1], P('grp'), parts along dimension 0, may hold values from 0 to 3; in each aligned block of 32 rows (0 to 31, 32 to 63, ..., all dimensions but the last counted through in order) at most 16 rows name the same one
- sub_sector: int32 [16, 16], P('grp'), parts along dimension 0, may hold values from 0 to 1
Outputs:
- sigma: bfloat16 [16, 16, 128, 128], P(('grp', 'sec'), None, 'term'), parts along dimension 0
The draws below stay inside these ranges and needn't reach their ends.
There are 2 independent parts, one for each index of `grp`. The reference program is written for one: setup_inputs(seed, part) draws one part's arguments, and reference() takes and returns one part's arrays. A program takes and returns all parts, laid end to end along the dimension named above; each array names one. Nothing has to cross between parts.
Inputs may be any that keep to these rules, and one draw needn't show every extreme that they name: `dest_owner`: among the 32 blocks of one device (right sectors in order), no owner is named more than 16 times, a bound that some block reaches.
All inputs are finite; a program needn't handle non-finite values.
Results may differ from the reference program's by a relative error of at most 0.0049.
Values may be sent and summed in bfloat16 or wider, within the bound.
A program may use at most 128 MiB of HBM per device.

```python
import math
import jax
import jax.numpy as jnp
import numpy as np
from jax import lax

BLK = 128
K = 16
SEC_DEV = 2
TERMS = 24
NSEC = 8
CAP = 16
N_SEC = 4


def touch_ends(array, rng, low, largest):
    longest = array.shape.index(max(array.shape))
    spots = []
    for shift in (0, 1):
        where = [jax.random.randint(jax.random.fold_in(rng, axis), (), 0, length) for axis, length in enumerate(array.shape)]
        where[longest] = (where[longest] + shift) % array.shape[longest]
        spots.append(tuple(where))
    return array.at[spots[0]].set(low).at[spots[1]].set(largest)


def level_of(key, extent, cuts, least, largest):
    gain = 1.0
    for axis_at, parts in cuts:
        steps = jax.random.uniform(jax.random.fold_in(jax.random.fold_in(key, 6), axis_at), (parts,), jnp.float32, least / len(cuts), largest / len(cuts))
        gain = gain * jnp.repeat(jnp.exp(steps), extent[axis_at] // parts).reshape((-1,) + (1,) * (len(extent) - 1 - axis_at))
    return gain


def shared_out(own_key, own, number, rows, amount, top, bound, slope):
    ranking = jax.random.permutation(own_key, amount)
    packed, ordinary = portions_of(amount, rows * top, bound, slope, True), portions_of(amount, rows * top, bound, slope, False)
    places = jnp.arange(amount)

    def named(tallies, turn):
        used = int((tallies > 0).sum())
        fixed = max(1, used // 4)
        moved = fixed + (places - fixed + turn * (used - fixed)) % max(1, amount - fixed)
        return jnp.zeros((amount,), jnp.int32).at[ranking[jnp.where(places < fixed, places, moved)]].set(jnp.asarray(tallies, jnp.int32))

    tallies = jnp.where(number % 4 == 0, named(packed, number // 4), named(ordinary, number - number // 4 - 1))
    mixed = jax.random.permutation(jax.random.fold_in(own, 3), amount)
    donor, sink = mixed[0:amount // 2 * 2:2], mixed[1:amount // 2 * 2:2]
    slack = jnp.minimum(tallies[donor] - 1, bound - tallies[sink]) // 2
    slack = jnp.where((donor == ranking[0]) | (sink == ranking[0]) | (tallies[sink] == 0), 0, jnp.maximum(slack, 0))
    moved = jax.random.randint(jax.random.fold_in(own, 4), (amount // 2,), 0, 1 << 20) % (slack + 1)
    tallies = tallies.at[donor].add(-moved).at[sink].add(moved)
    members = jnp.searchsorted(jnp.cumsum(tallies), jnp.arange(rows * top), side="right").astype(jnp.int32)
    listing = members.reshape(top, rows).T
    listing = listing[jax.random.permutation(jax.random.fold_in(own, 1), rows)]
    turn = jax.random.randint(jax.random.fold_in(own, 2), (rows, 1), 0, top)
    return jnp.take_along_axis(listing, (jnp.arange(top)[None, :] + turn) % top, axis=1)


def portions_of(amount, total, most, lean, full):
    portions = [(1 << 20) // math.isqrt(grade ** lean) + 1 for grade in range(1, amount + 1)]
    largest = most if full else min(most, max(-(-total // amount), total * portions[0] // sum(portions)))
    least = 1 if total - largest >= amount - 1 else 0
    holding, rest = [largest] + [least] * (amount - 1), total - largest - least * (amount - 1)
    while rest > 0:
        candidates = [i for i in range(1, amount) if holding[i] < largest] or [i for i in range(1, amount) if holding[i] < most]
        mass, left = sum([portions[i] for i in candidates]), rest
        for i in candidates:
            addition = min(most - holding[i], max(1, left * portions[i] // mass), rest)
            holding[i] = holding[i] + addition
            rest = rest - addition
    return np.array(holding)


def scatter_about(rng, extent, scale, bound, pieces=(), held_as=jnp.bfloat16):
    array = jax.random.normal(rng, extent, jnp.float32) * scale
    if len(pieces) > 0:
        array = level_of(rng, extent, pieces, -0.22, 0.18) * array
    return jnp.clip(array, min=-bound, max=bound).astype(held_as)


def setup_inputs(seed: int = 0, part: int = 0) -> dict:
    streams_of = jax.random.split(jax.random.key(seed), 7)
    own_keys = jax.random.split(jax.random.fold_in(streams_of[6], part), 7)
    wave_blocks = scatter_about(own_keys[0], (NSEC, K, BLK, BLK), 1.0, 6.0, ((0, 4),))
    right_env = scatter_about(own_keys[1], (TERMS, NSEC, BLK, BLK), BLK ** -0.5, 0.5, ((0, 4), (1, 4)))
    left_env = scatter_about(own_keys[2], (TERMS, NSEC, BLK, BLK), BLK ** -0.5, 0.5, ((0, 4), (1, 4)))
    site_coeff = jnp.clip(jax.random.uniform(own_keys[3], (TERMS, K), jnp.float32, -0.4, 0.4) * level_of(own_keys[3], (TERMS, K), ((0, 4),), -0.4, 0.0), -0.4, 0.4)
    dest_owner_keys = jax.random.split(jax.random.fold_in(own_keys[4], 1), NSEC * K // (SEC_DEV * K))
    dest_owner_turns = jax.random.permutation(jax.random.fold_in(own_keys[4], 3), NSEC * K // (SEC_DEV * K))
    dest_owner = jax.vmap(lambda own, number: shared_out(jax.random.fold_in(own_keys[4], 2), own, number, SEC_DEV * K, N_SEC, 1, CAP, 2))(dest_owner_keys, dest_owner_turns).reshape((NSEC, K, 1))
    sub_sector = touch_ends(jax.random.randint(own_keys[5], (NSEC, K), 0, SEC_DEV), jax.random.fold_in(own_keys[5], 1), 0, SEC_DEV - 1).astype(jnp.int32)
    return {"wave_blocks": wave_blocks, "right_env": right_env, "left_env": left_env, "site_coeff": site_coeff, "dest_owner": dest_owner, "sub_sector": sub_sector}


def reference(wave_blocks, right_env, left_env, site_coeff, dest_owner, sub_sector):
    left_sector = (dest_owner[:, :, 0] * SEC_DEV + sub_sector).astype(jnp.int32)
    right_by_sector = jnp.swapaxes(right_env, 0, 1)

    def one_sector(inputs):
        blocks, rights, lefts = inputs
        product = jnp.einsum('sab,tbc->tsac', blocks.astype(jnp.float32), rights.astype(jnp.float32))
        wave = (product * site_coeff[:, :, None, None]).astype(jnp.bfloat16)
        chosen = jnp.take(left_env, lefts, axis=1)
        result = jnp.einsum('tsab,tsbc->sac', chosen.astype(jnp.float32), wave.astype(jnp.float32))
        return result.astype(jnp.bfloat16)

    return lax.map(one_sector, (wave_blocks, right_by_sector, left_sector))
```

```python
import functools

import jax
import jax.numpy as jnp
from jax import lax
from jax.experimental import pallas as pl
from jax.experimental.pallas import tpu as pltpu
from jax.sharding import PartitionSpec as P

MESH = pl.DeviceIdType.MESH
GROUPS = 4


def body(
    n, nt, tc, sd, phys, side, nterm,
    wb_hbm, r_hbm, l_hbm, coeff, owner_ref, sub_ref, out_ref,
    wb, rcat, acc, s1, r1, s2, r2, *rest,
):
    nch = nt // tc
    gath, wave = rest[:nch], rest[nch:2 * nch]
    load_sem, lsem, rl_sem, send_r, send_l, recv, ssem1, rsem1, ssem2, rsem2 = rest[2 * nch:]
    g, i, t = lax.axis_index("grp"), lax.axis_index("sec"), lax.axis_index("term")
    q_all = sd * phys
    qg = q_all // GROUPS
    rows = side // nterm
    half = nterm // 2
    low = lax.rem(t, 2)
    high = t // 2
    pair = t + 1 - 2 * low
    across = lax.rem(t + half, nterm)
    has_r, has_l = i < n - 1, i > 0
    right, left = (g, jnp.minimum(i + 1, n - 1), t), (g, jnp.maximum(i - 1, 0), t)

    wb_load = pltpu.make_async_copy(wb_hbm, wb, load_sem)
    wb_load.start()
    r_loads = []
    for k in range(nt):
        for r in range(sd):
            cp = pltpu.make_async_copy(
                r_hbm.at[k, r], rcat.at[r, k // tc, :, pl.ds((k % tc) * side, side)], rl_sem.at[k, r]
            )
            cp.start()
            r_loads.append(cp)
    own_loads = []
    for c in range(nch):
        cp = pltpu.make_async_copy(l_hbm.at[pl.ds(c * tc, tc)], gath[c].at[i], lsem.at[c])
        cp.start()
        own_loads.append(cp)

    barrier = pltpu.get_barrier_semaphore()

    @pl.when(has_r)
    def _():
        pl.semaphore_signal(barrier, inc=1, device_id=right, device_id_type=MESH)

    @pl.when(has_l)
    def _():
        pl.semaphore_signal(barrier, inc=1, device_id=left, device_id_type=MESH)

    for peer in (pair, across):
        pl.semaphore_signal(barrier, inc=1, device_id=(g, i, peer), device_id_type=MESH)
    pl.semaphore_wait(barrier, 2 + has_r.astype(jnp.int32) + has_l.astype(jnp.int32))

    def piece(c, origin, to_right, own):
        dst = gath[c].at[origin]
        src = l_hbm.at[pl.ds(c * tc, tc)] if own else dst
        return pltpu.make_async_remote_copy(
            src_ref=src, dst_ref=dst,
            send_sem=(send_r if to_right else send_l).at[c, origin],
            recv_sem=recv.at[c, origin],
            device_id=right if to_right else left, device_id_type=MESH,
        )

    for c in range(nch):
        @pl.when(has_r)
        def _(c=c):
            piece(c, i, True, True).start()

        @pl.when(has_l)
        def _(c=c):
            piece(c, i, False, True).start()

    def relay(s, c):
        from_l, from_r = i - 1 - s, i + 1 + s

        @pl.when(from_l >= 0)
        def _():
            piece(c, from_l, True, False).wait_recv()

            @pl.when(has_r)
            def _():
                piece(c, from_l, True, False).start()

        @pl.when(from_r <= n - 1)
        def _():
            piece(c, from_r, False, False).wait_recv()

            @pl.when(has_l)
            def _():
                piece(c, from_r, False, False).start()

    wb_load.wait()
    for cp in r_loads:
        cp.wait()

    def wave_part(r, lo, hi):
        def step(k, _):
            for c in range(nch):
                s0 = 2 * k
                lhs = wb[r, pl.ds(s0, 2)].reshape(2 * side, side)
                prod = jnp.dot(lhs, rcat[r, c], preferred_element_type=jnp.float32)
                for j in range(2):
                    for u in range(tc):
                        scaled = prod[j * side:(j + 1) * side, u * side:(u + 1) * side] * coeff[c * tc + u, s0 + j]
                        wave[c][r * phys + s0 + j, u * side:(u + 1) * side, :] = scaled.astype(jnp.bfloat16)
            return 0

        lax.fori_loop(lo, hi, step, 0)

    def product(c, q):
        r, s = q // phys, lax.rem(q, phys)
        own, sub = owner_ref[i * sd + r, s], sub_ref[i * sd + r, s]
        lhs = jnp.concatenate([gath[c][own, u, sub] for u in range(tc)], axis=1)
        return jnp.dot(lhs, wave[c][q], preferred_element_type=jnp.float32)

    pairs = phys // 2
    wave_part(0, 0, pairs)
    wave_part(1, 0, pairs // 2)
    for r in range(2, sd):
        wave_part(r, 0, pairs)
    if n > 2:
        relay(0, 0)
    wave_part(1, pairs // 2, pairs)
    if n > 2:
        for c in range(1, nch):
            relay(0, c)
        def steps(s, _):
            for c in range(nch):
                relay(s, c)
            return 0
        lax.fori_loop(1, n - 2, steps, 0)
    for cp in own_loads:
        cp.wait()

    for c in range(nch - 1):
        relay(n - 2, c)

        def add(q, _, c=c):
            p = product(c, q)
            acc[q] = p if c == 0 else acc[q] + p
            return 0

        lax.fori_loop(0, q_all, add, 0, unroll=2)
    last = nch - 1
    relay(n - 2, last)

    def hop1(k):
        return pltpu.make_async_remote_copy(
            src_ref=s1.at[k], dst_ref=r1.at[k], send_sem=ssem1.at[k], recv_sem=rsem1.at[k],
            device_id=(g, i, pair), device_id_type=MESH,
        )

    def hop2(k):
        return pltpu.make_async_remote_copy(
            src_ref=s2.at[k], dst_ref=r2.at[k], send_sem=ssem2.at[k], recv_sem=rsem2.at[k],
            device_id=(g, i, across), device_id_type=MESH,
        )

    def rows_of(dest):
        return pl.ds(pl.multiple_of(dest * rows, rows), rows)

    def middle(k):
        hop1(k).wait_recv()

        def one(j, _):
            q = k * qg + j
            away = acc[q, rows_of((1 - high) * 2 + low)] + r1[k, j, 1 - high].astype(jnp.float32)
            s2[k, j] = away.astype(jnp.bfloat16)
            return 0

        lax.fori_loop(0, qg, one, 0, unroll=4)
        hop2(k).start()

    for k in range(GROUPS):
        def finish(j, _, k=k):
            q = k * qg + j
            acc[q] = acc[q] + product(last, q)
            for h in range(half):
                s1[k, j, h] = acc[q, rows_of(2 * h + 1 - low)].astype(jnp.bfloat16)
            return 0

        lax.fori_loop(0, qg, finish, 0, unroll=2)
        hop1(k).start()
        if k >= 1:
            middle(k - 1)
    middle(GROUPS - 1)
    for k in range(GROUPS):
        hop2(k).wait_recv()

        def close(j, _, k=k):
            q = k * qg + j
            mine = acc[q, rows_of(t)] + r1[k, j, high].astype(jnp.float32)
            total = mine + r2[k, j].astype(jnp.float32)
            out_ref[q // phys, lax.rem(q, phys)] = total.astype(jnp.bfloat16)
            return 0

        lax.fori_loop(0, qg, close, 0, unroll=4)

    for k in range(GROUPS):
        hop1(k).wait_send()
        hop2(k).wait_send()

    def drain(o, _):
        for c in range(nch):
            @pl.when(jnp.logical_and(has_r, o <= i))
            def _(c=c):
                piece(c, o, True, False).wait_send()

            @pl.when(jnp.logical_and(has_l, o >= i))
            def _(c=c):
                piece(c, o, False, False).wait_send()
        return 0

    lax.fori_loop(0, n, drain, 0)


def local(n, nterm, wave_blocks, right_env, left_env, site_coeff, dest_owner, sub_sector):
    sd, phys, side, _ = wave_blocks.shape
    nt = right_env.shape[0]
    tc = 2 if nt % 2 == 0 else 1
    nch = nt // tc
    rows, half, qg = side // nterm, nterm // 2, sd * phys // GROUPS
    bf, dma = jnp.bfloat16, pltpu.SemaphoreType.DMA
    anywhere, smem = pl.BlockSpec(memory_space=pl.ANY), pl.BlockSpec(memory_space=pltpu.SMEM)
    flops = 4 * nt * sd * phys * side ** 3
    return pl.pallas_call(
        functools.partial(body, n, nt, tc, sd, phys, side, nterm),
        out_shape=jax.ShapeDtypeStruct((sd, phys, rows, side), bf),
        in_specs=[anywhere] * 3 + [smem] * 3,
        out_specs=pl.BlockSpec(memory_space=pltpu.VMEM),
        scratch_shapes=[
            pltpu.VMEM((sd, phys, side, side), bf),
            pltpu.VMEM((sd, nch, side, tc * side), bf),
            pltpu.VMEM((sd * phys, side, side), jnp.float32),
            pltpu.VMEM((GROUPS, qg, half, rows, side), bf),
            pltpu.VMEM((GROUPS, qg, half, rows, side), bf),
            pltpu.VMEM((GROUPS, qg, rows, side), bf),
            pltpu.VMEM((GROUPS, qg, rows, side), bf),
        ]
        + [pltpu.VMEM((n, tc, sd, side, side), bf)] * nch
        + [pltpu.VMEM((sd * phys, tc * side, side), bf)] * nch
        + [dma, dma((nch,)), dma((nt, sd)), dma((nch, n)), dma((nch, n)), dma((nch, n))]
        + [dma((GROUPS,))] * 4,
        compiler_params=pltpu.CompilerParams(
            collective_id=0, has_side_effects=True, vmem_limit_bytes=52 << 20
        ),
        cost_estimate=pl.CostEstimate(flops=flops, bytes_accessed=4 << 20, transcendentals=0),
        name="sigma",
    )(wave_blocks, right_env, left_env, site_coeff, dest_owner.reshape(sub_sector.shape), sub_sector)


def solution(mesh):
    placed = (
        P(("grp", "sec"), None, None, None),
        P(("grp", "term"), "sec", None, None),
        P(("grp", "term"), "sec", None, None),
        P(("grp", "term"), None),
        P("grp", None, None),
        P("grp", None),
    )
    return jax.shard_map(
        functools.partial(local, mesh.shape["sec"], mesh.shape["term"]),
        mesh=mesh,
        in_specs=placed,
        out_specs=P(("grp", "sec"), None, "term", None),
        check_vma=False,
    )
```

```python
import functools

import jax
import jax.numpy as jnp
from jax import lax
from jax.experimental import pallas as pl
from jax.experimental.pallas import tpu as pltpu
from jax.sharding import PartitionSpec as P

MESH = pl.DeviceIdType.MESH
GROUPS = 4


def body(
    n, nt, tc, sd, phys, side, nterm,
    wb_hbm, r_hbm, l_hbm, coeff_hbm, owner_hbm, sub_hbm, out_ref,
    coeff, owner_ref, sub_ref, coeff_x, coeff_v, small_sem, wb, rcat, rcat_x, acc, bacc, s1, r1, s2, r2, s3, r3, *rest,
):
    nch = nt // tc
    gath, wave = rest[:nch], rest[nch:2 * nch]
    load_sem, lsem, rl_sem, send_r, send_l, recv, ssem1, rsem1, ssem2, rsem2, ssem3, rsem3, xs, xr = rest[2 * nch:]
    last = nch - 1
    hr = side // 2
    g, i, t = lax.axis_index("grp"), lax.axis_index("sec"), lax.axis_index("term")
    q_all = sd * phys
    qg = q_all // GROUPS
    rows = side // nterm
    half = nterm // 2
    low = lax.rem(t, 2)
    high = t // 2
    pair = t + 1 - 2 * low
    across = lax.rem(t + half, nterm)
    has_r, has_l = i < n - 1, i > 0
    right, left = (g, jnp.minimum(i + 1, n - 1), t), (g, jnp.maximum(i - 1, 0), t)

    wb_load = pltpu.make_async_copy(wb_hbm, wb, load_sem)
    wb_load.start()
    small_loads = [
        pltpu.make_async_copy(src, dst, small_sem.at[k])
        for k, (src, dst) in enumerate(((coeff_hbm, coeff), (owner_hbm, owner_ref), (sub_hbm, sub_ref)))
    ]
    for cp in small_loads:
        cp.start()
    r_loads = []
    for k in range(nt):
        for r in range(sd):
            cp = pltpu.make_async_copy(
                r_hbm.at[k, r], rcat.at[r, k // tc, :, pl.ds((k % tc) * side, side)], rl_sem.at[k, r]
            )
            cp.start()
            r_loads.append(cp)
    own_loads = []
    for c in range(nch):
        if c == last:
            my_rows = pl.ds(pl.multiple_of(high * hr, hr), hr)
            cp = pltpu.make_async_copy(
                l_hbm.at[pl.ds(c * tc, tc), :, my_rows], gath[c].at[i, 0], lsem.at[c]
            )
        else:
            cp = pltpu.make_async_copy(l_hbm.at[pl.ds(c * tc, tc)], gath[c].at[i], lsem.at[c])
        cp.start()
        own_loads.append(cp)

    barrier = pltpu.get_barrier_semaphore()

    @pl.when(has_r)
    def _():
        pl.semaphore_signal(barrier, inc=1, device_id=right, device_id_type=MESH)

    @pl.when(has_l)
    def _():
        pl.semaphore_signal(barrier, inc=1, device_id=left, device_id_type=MESH)

    for peer in (pair, across):
        pl.semaphore_signal(barrier, inc=1, device_id=(g, i, peer), device_id_type=MESH)
    pl.semaphore_wait(barrier, 2 + has_r.astype(jnp.int32) + has_l.astype(jnp.int32))

    def piece(c, origin, to_right, own):
        dst = gath[c].at[origin]
        src = l_hbm.at[pl.ds(c * tc, tc)] if own and c != last else dst
        return pltpu.make_async_remote_copy(
            src_ref=src, dst_ref=dst,
            send_sem=(send_r if to_right else send_l).at[c, origin],
            recv_sem=recv.at[c, origin],
            device_id=right if to_right else left, device_id_type=MESH,
        )

    def send_own(c):
        @pl.when(has_r)
        def _():
            piece(c, i, True, True).start()

        @pl.when(has_l)
        def _():
            piece(c, i, False, True).start()

    send_own(0)

    def swap(k, src, dst):
        return pltpu.make_async_remote_copy(
            src_ref=src, dst_ref=dst, send_sem=xs.at[k], recv_sem=xr.at[k],
            device_id=(g, i, across), device_id_type=MESH,
        )

    their_rows = pl.ds(pl.multiple_of((1 - high) * hr, hr), hr)
    swap_l = swap(0, l_hbm.at[pl.ds(last * tc, tc), :, their_rows], gath[last].at[i, 1])
    swap_c = swap(1, coeff_hbm, coeff_v)
    swap_r = [
        swap(2 + u * sd + r, r_hbm.at[last * tc + u, r], rcat_x.at[r, :, pl.ds(u * side, side)])
        for u in range(tc) for r in range(sd)
    ]
    swaps = [swap_l, swap_c] + swap_r
    for cp in swaps:
        cp.start()
    for c in range(1, last):
        send_own(c)

    def relay(s, c):
        from_l, from_r = i - 1 - s, i + 1 + s

        @pl.when(from_l >= 0)
        def _():
            piece(c, from_l, True, False).wait_recv()

            @pl.when(has_r)
            def _():
                piece(c, from_l, True, False).start()

        @pl.when(from_r <= n - 1)
        def _():
            piece(c, from_r, False, False).wait_recv()

            @pl.when(has_l)
            def _():
                piece(c, from_r, False, False).start()

    wb_load.wait()
    for cp in small_loads:
        cp.wait()
    for cp in r_loads:
        cp.wait()

    def wave_part(r, lo, hi, theirs=False):
        def step(k, _):
            for c in (last,) if theirs else range(nch):
                s0 = 2 * k
                lhs = wb[r, pl.ds(s0, 2)].reshape(2 * side, side)
                rhs = rcat_x[r] if theirs else rcat[r, c]
                prod = jnp.dot(lhs, rhs, preferred_element_type=jnp.float32)
                for j in range(2):
                    for u in range(tc):
                        scale = (coeff_x if theirs else coeff)[c * tc + u, s0 + j]
                        scaled = prod[j * side:(j + 1) * side, u * side:(u + 1) * side] * scale
                        at = (u + (tc if theirs else 0)) * side
                        wave[c][r * phys + s0 + j, at:at + side, :] = scaled.astype(jnp.bfloat16)
            return 0

        lax.fori_loop(lo, hi, step, 0)

    def product(c, q):
        r, s = q // phys, lax.rem(q, phys)
        own, sub = owner_ref[i * sd + r, s], sub_ref[i * sd + r, s]
        if c == last:
            parts = [gath[c][own, h, u, sub] for h in range(2) for u in range(tc)]
        else:
            parts = [gath[c][own, u, sub] for u in range(tc)]
        lhs = jnp.concatenate(parts, axis=1)
        return jnp.dot(lhs, wave[c][q], preferred_element_type=jnp.float32)

    pairs = phys // 2
    wave_part(0, 0, pairs)
    if n > 2:
        relay(0, 0)
    for r in range(1, sd):
        wave_part(r, 0, pairs)
    if n > 2:
        for c in range(1, last):
            relay(0, c)
    for cp in swaps:
        cp.wait_recv()
    to_scalar = pltpu.make_async_copy(coeff_v, coeff_x, small_sem.at[3])
    to_scalar.start()
    to_scalar.wait()
    for r in range(sd):
        wave_part(r, 0, pairs, True)

    def steps(s, _):
        for c in range(last):
            relay(s, c)
        return 0

    if n > 3:
        lax.fori_loop(1, n - 2, steps, 0)
    for cp in own_loads:
        cp.wait()
    send_own(last)

    for c in range(last - 1):
        relay(n - 2, c)

        def add(q, _, c=c):
            p = product(c, q)
            acc[q] = p if c == 0 else acc[q] + p
            return 0

        lax.fori_loop(0, q_all, add, 0, unroll=2)
    relay(n - 2, last - 1)

    def hop1(k):
        return pltpu.make_async_remote_copy(
            src_ref=s1.at[k], dst_ref=r1.at[k], send_sem=ssem1.at[k], recv_sem=rsem1.at[k],
            device_id=(g, i, pair), device_id_type=MESH,
        )

    def hop2(k):
        return pltpu.make_async_remote_copy(
            src_ref=s2.at[k], dst_ref=r2.at[k], send_sem=ssem2.at[k], recv_sem=rsem2.at[k],
            device_id=(g, i, across), device_id_type=MESH,
        )

    def hop3(k):
        return pltpu.make_async_remote_copy(
            src_ref=s3.at[k], dst_ref=r3.at[k], send_sem=ssem3.at[k], recv_sem=rsem3.at[k],
            device_id=(g, i, pair), device_id_type=MESH,
        )

    def rows_of(dest):
        return pl.ds(pl.multiple_of(dest * rows, rows), rows)

    def middle(k):
        hop1(k).wait_recv()

        def one(j, _):
            q = k * qg + j
            away = acc[q, rows_of((1 - high) * 2 + low)] + r1[k, j, 1 - high].astype(jnp.float32)
            s2[k, j] = away.astype(jnp.bfloat16)
            return 0

        lax.fori_loop(0, qg, one, 0, unroll=4)
        hop2(k).start()

    for k in range(GROUPS):
        def finish(j, _, k=k):
            q = k * qg + j
            p = product(last - 1, q)
            acc[q] = p if last == 1 else acc[q] + p
            for h in range(half):
                s1[k, j, h] = acc[q, rows_of(2 * h + 1 - low)].astype(jnp.bfloat16)
            return 0

        lax.fori_loop(0, qg, finish, 0, unroll=2)
        hop1(k).start()
        if k >= 1:
            middle(k - 1)
    middle(GROUPS - 1)

    def tail_steps(s, _):
        relay(s, last)
        return 0

    lax.fori_loop(0, n - 1, tail_steps, 0)
    for k in range(GROUPS):
        def tail(j, _, k=k):
            q = k * qg + j
            bacc[q] = product(last, q)
            s3[k, j] = bacc[q, rows_of(1 - low)].astype(jnp.bfloat16)
            return 0

        lax.fori_loop(0, qg, tail, 0, unroll=2)
        hop3(k).start()
    for k in range(GROUPS):
        hop2(k).wait_recv()
        hop3(k).wait_recv()

        def close(j, _, k=k):
            q = k * qg + j
            mine = acc[q, rows_of(t)] + r1[k, j, high].astype(jnp.float32)
            total = mine + r2[k, j].astype(jnp.float32)
            total = total + bacc[q, rows_of(low)] + r3[k, j].astype(jnp.float32)
            out_ref[q // phys, lax.rem(q, phys)] = total.astype(jnp.bfloat16)
            return 0

        lax.fori_loop(0, qg, close, 0, unroll=4)

    for k in range(GROUPS):
        hop1(k).wait_send()
        hop2(k).wait_send()
        hop3(k).wait_send()
    for cp in swaps:
        cp.wait_send()

    def drain(o, _):
        for c in range(nch):
            @pl.when(jnp.logical_and(has_r, o <= i))
            def _(c=c):
                piece(c, o, True, False).wait_send()

            @pl.when(jnp.logical_and(has_l, o >= i))
            def _(c=c):
                piece(c, o, False, False).wait_send()
        return 0

    lax.fori_loop(0, n, drain, 0)


def local(n, nterm, wave_blocks, right_env, left_env, site_coeff, dest_owner, sub_sector):
    sd, phys, side, _ = wave_blocks.shape
    nt = right_env.shape[0]
    tc = 2 if nt % 2 == 0 else 1
    nch = nt // tc
    rows, half, qg = side // nterm, nterm // 2, sd * phys // GROUPS
    bf, dma = jnp.bfloat16, pltpu.SemaphoreType.DMA
    hbm = pl.BlockSpec(memory_space=pltpu.HBM)
    flops = 4 * nt * sd * phys * side ** 3
    return pl.pallas_call(
        functools.partial(body, n, nt, tc, sd, phys, side, nterm),
        out_shape=jax.ShapeDtypeStruct((sd, phys, rows, side), bf),
        in_specs=[hbm] * 6,
        out_specs=pl.BlockSpec(memory_space=pltpu.VMEM),
        scratch_shapes=[
            pltpu.SMEM(site_coeff.shape, jnp.float32),
            pltpu.SMEM(sub_sector.shape, jnp.int32),
            pltpu.SMEM(sub_sector.shape, jnp.int32),
            pltpu.SMEM(site_coeff.shape, jnp.float32),
            pltpu.VMEM(site_coeff.shape, jnp.float32),
            dma((4,)),
            pltpu.VMEM((sd, phys, side, side), bf),
            pltpu.VMEM((sd, nch, side, tc * side), bf),
            pltpu.VMEM((sd, side, tc * side), bf),
            pltpu.VMEM((sd * phys, side, side), jnp.float32),
            pltpu.VMEM((sd * phys, side // 2, side), jnp.float32),
            pltpu.VMEM((GROUPS, qg, half, rows, side), bf),
            pltpu.VMEM((GROUPS, qg, half, rows, side), bf),
        ]
        + [pltpu.VMEM((GROUPS, qg, rows, side), bf)] * 4
        + [pltpu.VMEM((n, tc, sd, side, side), bf)] * (nch - 1)
        + [pltpu.VMEM((n, 2, tc, sd, side // 2, side), bf)]
        + [pltpu.VMEM((sd * phys, tc * side, side), bf)] * (nch - 1)
        + [pltpu.VMEM((sd * phys, 2 * tc * side, side), bf)]
        + [dma, dma((nch,)), dma((nt, sd)), dma((nch, n)), dma((nch, n)), dma((nch, n))]
        + [dma((GROUPS,))] * 6
        + [dma((2 + tc * sd,))] * 2,
        compiler_params=pltpu.CompilerParams(
            collective_id=0, has_side_effects=True, vmem_limit_bytes=63 << 20
        ),
        cost_estimate=pl.CostEstimate(flops=flops, bytes_accessed=4 << 20, transcendentals=0),
        name="sigma",
    )(wave_blocks, right_env, left_env, site_coeff, dest_owner.reshape(sub_sector.shape), sub_sector)


def solution(mesh):
    placed = (
        P(("grp", "sec"), None, None, None),
        P(("grp", "term"), "sec", None, None),
        P(("grp", "term"), "sec", None, None),
        P(("grp", "term"), None),
        P("grp", None, None),
        P("grp", None),
    )
    return jax.shard_map(
        functools.partial(local, mesh.shape["sec"], mesh.shape["term"]),
        mesh=mesh,
        in_specs=placed,
        out_specs=P(("grp", "sec"), None, "term", None),
        check_vma=False,
    )
```

```python
import functools

import jax
import jax.numpy as jnp
from jax import lax
from jax.experimental import pallas as pl
from jax.experimental.pallas import tpu as pltpu
from jax.sharding import PartitionSpec as P

MESH = pl.DeviceIdType.MESH
GROUPS = 4


def body(
    n, nt, tc, sd, phys, side, nterm,
    wb_hbm, r_hbm, l_hbm, coeff_hbm, owner_hbm, sub_hbm, out_ref,
    coeff, owner_ref, sub_ref, coeff_x, coeff_v, small_sem, wb, rcat, rcat_x, acc, bacc, s1, r1, s2, r2, s3, r3, *rest,
):
    nch = nt // tc
    gath, wave = rest[:nch], rest[nch:2 * nch]
    load_sem, lsem, rl_sem, send_r, send_l, recv, ssem1, rsem1, ssem2, rsem2, ssem3, rsem3, xs, xr = rest[2 * nch:]
    last = nch - 1
    hr = side // 2
    g, i, t = lax.axis_index("grp"), lax.axis_index("sec"), lax.axis_index("term")
    q_all = sd * phys
    qg = q_all // GROUPS
    rows = side // nterm
    half = nterm // 2
    low = lax.rem(t, 2)
    high = t // 2
    pair = t + 1 - 2 * low
    across = lax.rem(t + half, nterm)
    has_r, has_l = i < n - 1, i > 0
    right, left = (g, jnp.minimum(i + 1, n - 1), t), (g, jnp.maximum(i - 1, 0), t)

    wb_load = pltpu.make_async_copy(wb_hbm, wb, load_sem)
    wb_load.start()
    small_loads = [
        pltpu.make_async_copy(src, dst, small_sem.at[k])
        for k, (src, dst) in enumerate(((coeff_hbm, coeff), (owner_hbm, owner_ref), (sub_hbm, sub_ref)))
    ]
    for cp in small_loads:
        cp.start()
    r_loads = []
    for k in range(nt):
        for r in range(sd):
            cp = pltpu.make_async_copy(
                r_hbm.at[k, r], rcat.at[r, k // tc, :, pl.ds((k % tc) * side, side)], rl_sem.at[k, r]
            )
            cp.start()
            r_loads.append(cp)
    own_loads = []
    for c in range(nch):
        if c == last:
            my_rows = pl.ds(pl.multiple_of(high * hr, hr), hr)
            cp = pltpu.make_async_copy(
                l_hbm.at[pl.ds(c * tc, tc), :, my_rows], gath[c].at[i, 0], lsem.at[c]
            )
        else:
            cp = pltpu.make_async_copy(l_hbm.at[pl.ds(c * tc, tc)], gath[c].at[i], lsem.at[c])
        cp.start()
        own_loads.append(cp)

    barrier = pltpu.get_barrier_semaphore()

    @pl.when(has_r)
    def _():
        pl.semaphore_signal(barrier, inc=1, device_id=right, device_id_type=MESH)

    @pl.when(has_l)
    def _():
        pl.semaphore_signal(barrier, inc=1, device_id=left, device_id_type=MESH)

    for peer in (pair, across):
        pl.semaphore_signal(barrier, inc=1, device_id=(g, i, peer), device_id_type=MESH)
    pl.semaphore_wait(barrier, 2 + has_r.astype(jnp.int32) + has_l.astype(jnp.int32))

    def piece(c, origin, to_right, own):
        dst = gath[c].at[origin]
        src = l_hbm.at[pl.ds(c * tc, tc)] if own and c != last else dst
        return pltpu.make_async_remote_copy(
            src_ref=src, dst_ref=dst,
            send_sem=(send_r if to_right else send_l).at[c, origin],
            recv_sem=recv.at[c, origin],
            device_id=right if to_right else left, device_id_type=MESH,
        )

    def send_own(c):
        @pl.when(has_r)
        def _():
            piece(c, i, True, True).start()

        @pl.when(has_l)
        def _():
            piece(c, i, False, True).start()

    send_own(0)

    def swap(k, src, dst):
        return pltpu.make_async_remote_copy(
            src_ref=src, dst_ref=dst, send_sem=xs.at[k], recv_sem=xr.at[k],
            device_id=(g, i, across), device_id_type=MESH,
        )

    their_rows = pl.ds(pl.multiple_of((1 - high) * hr, hr), hr)
    swap_l = swap(0, l_hbm.at[pl.ds(last * tc, tc), :, their_rows], gath[last].at[i, 1])
    swap_c = swap(1, coeff_hbm, coeff_v)
    swap_r = [
        swap(2 + u * sd + r, r_hbm.at[last * tc + u, r], rcat_x.at[r, :, pl.ds(u * side, side)])
        for u in range(tc) for r in range(sd)
    ]
    swaps = [swap_l, swap_c] + swap_r
    for cp in swaps:
        cp.start()
    for c in range(1, last):
        send_own(c)

    def relay(s, c):
        from_l, from_r = i - 1 - s, i + 1 + s

        @pl.when(from_l >= 0)
        def _():
            piece(c, from_l, True, False).wait_recv()

            @pl.when(has_r)
            def _():
                piece(c, from_l, True, False).start()

        @pl.when(from_r <= n - 1)
        def _():
            piece(c, from_r, False, False).wait_recv()

            @pl.when(has_l)
            def _():
                piece(c, from_r, False, False).start()

    wb_load.wait()
    for cp in small_loads:
        cp.wait()
    for cp in r_loads:
        cp.wait()

    def wave_part(r, lo, hi, theirs=False):
        def step(k, _):
            for c in (last,) if theirs else range(nch):
                s0 = 2 * k
                lhs = wb[r, pl.ds(s0, 2)].reshape(2 * side, side)
                rhs = rcat_x[r] if theirs else rcat[r, c]
                prod = jnp.dot(lhs, rhs, preferred_element_type=jnp.float32)
                for j in range(2):
                    for u in range(tc):
                        scale = (coeff_x if theirs else coeff)[c * tc + u, s0 + j]
                        scaled = prod[j * side:(j + 1) * side, u * side:(u + 1) * side] * scale
                        at = (u + (tc if theirs else 0)) * side
                        wave[c][r * phys + s0 + j, at:at + side, :] = scaled.astype(jnp.bfloat16)
            return 0

        lax.fori_loop(lo, hi, step, 0)

    def product(c, q):
        r, s = q // phys, lax.rem(q, phys)
        own, sub = owner_ref[i * sd + r, s], sub_ref[i * sd + r, s]
        if c == last:
            parts = [gath[c][own, h, u, sub] for h in range(2) for u in range(tc)]
        else:
            parts = [gath[c][own, u, sub] for u in range(tc)]
        lhs = jnp.concatenate(parts, axis=1)
        return jnp.dot(lhs, wave[c][q], preferred_element_type=jnp.float32)

    pairs = phys // 2
    wave_part(0, 0, pairs)
    if n > 2:
        relay(0, 0)
    for r in range(1, sd):
        wave_part(r, 0, pairs)
    if n > 2:
        for c in range(1, last):
            relay(0, c)
    for cp in swaps:
        cp.wait_recv()
    to_scalar = pltpu.make_async_copy(coeff_v, coeff_x, small_sem.at[3])
    to_scalar.start()
    to_scalar.wait()
    for r in range(sd):
        wave_part(r, 0, pairs, True)

    def steps(s, _):
        for c in range(last):
            relay(s, c)
        return 0

    if n > 3:
        lax.fori_loop(1, n - 2, steps, 0)
    for cp in own_loads:
        cp.wait()
    send_own(last)

    for c in range(last - 1):
        relay(n - 2, c)

        def add(q, _, c=c):
            p = product(c, q)
            acc[q] = p if c == 0 else acc[q] + p
            return 0

        lax.fori_loop(0, q_all, add, 0, unroll=4)
    relay(n - 2, last - 1)

    def hop1(k):
        return pltpu.make_async_remote_copy(
            src_ref=s1.at[k], dst_ref=r1.at[k], send_sem=ssem1.at[k], recv_sem=rsem1.at[k],
            device_id=(g, i, pair), device_id_type=MESH,
        )

    def hop2(k):
        return pltpu.make_async_remote_copy(
            src_ref=s2.at[k], dst_ref=r2.at[k], send_sem=ssem2.at[k], recv_sem=rsem2.at[k],
            device_id=(g, i, across), device_id_type=MESH,
        )

    def hop3(k):
        return pltpu.make_async_remote_copy(
            src_ref=s3.at[k], dst_ref=r3.at[k], send_sem=ssem3.at[k], recv_sem=rsem3.at[k],
            device_id=(g, i, pair), device_id_type=MESH,
        )

    def rows_of(dest):
        return pl.ds(pl.multiple_of(dest * rows, rows), rows)

    def middle(k):
        hop1(k).wait_recv()

        def one(j, _):
            q = k * qg + j
            away = acc[q, rows_of((1 - high) * 2 + low)] + r1[k, j, 1 - high].astype(jnp.float32)
            s2[k, j] = away.astype(jnp.bfloat16)
            return 0

        lax.fori_loop(0, qg, one, 0, unroll=4)
        hop2(k).start()

    for k in range(GROUPS):
        def finish(j, _, k=k):
            q = k * qg + j
            p = product(last - 1, q)
            acc[q] = p if last == 1 else acc[q] + p
            for h in range(half):
                s1[k, j, h] = acc[q, rows_of(2 * h + 1 - low)].astype(jnp.bfloat16)
            return 0

        lax.fori_loop(0, qg, finish, 0, unroll=4)
        hop1(k).start()
        if k >= 1:
            middle(k - 1)
    middle(GROUPS - 1)

    def tail_steps(s, _):
        relay(s, last)
        return 0

    lax.fori_loop(0, n - 1, tail_steps, 0)
    for k in range(GROUPS):
        def tail(j, _, k=k):
            q = k * qg + j
            bacc[q] = product(last, q)
            s3[k, j] = bacc[q, rows_of(1 - low)].astype(jnp.bfloat16)
            return 0

        lax.fori_loop(0, qg, tail, 0, unroll=8)
        hop3(k).start()
    for k in range(GROUPS):
        hop2(k).wait_recv()
        hop3(k).wait_recv()

        def close(j, _, k=k):
            q = k * qg + j
            mine = acc[q, rows_of(t)] + r1[k, j, high].astype(jnp.float32)
            total = mine + r2[k, j].astype(jnp.float32)
            total = total + bacc[q, rows_of(low)] + r3[k, j].astype(jnp.float32)
            out_ref[q // phys, lax.rem(q, phys)] = total.astype(jnp.bfloat16)
            return 0

        lax.fori_loop(0, qg, close, 0, unroll=8)

    for k in range(GROUPS):
        hop1(k).wait_send()
        hop2(k).wait_send()
        hop3(k).wait_send()
    for cp in swaps:
        cp.wait_send()

    def drain(o, _):
        for c in range(nch):
            @pl.when(jnp.logical_and(has_r, o <= i))
            def _(c=c):
                piece(c, o, True, False).wait_send()

            @pl.when(jnp.logical_and(has_l, o >= i))
            def _(c=c):
                piece(c, o, False, False).wait_send()
        return 0

    lax.fori_loop(0, n, drain, 0)


def local(n, nterm, wave_blocks, right_env, left_env, site_coeff, dest_owner, sub_sector):
    sd, phys, side, _ = wave_blocks.shape
    nt = right_env.shape[0]
    tc = 2 if nt % 2 == 0 else 1
    nch = nt // tc
    rows, half, qg = side // nterm, nterm // 2, sd * phys // GROUPS
    bf, dma = jnp.bfloat16, pltpu.SemaphoreType.DMA
    hbm = pl.BlockSpec(memory_space=pltpu.HBM)
    flops = 4 * nt * sd * phys * side ** 3
    return pl.pallas_call(
        functools.partial(body, n, nt, tc, sd, phys, side, nterm),
        out_shape=jax.ShapeDtypeStruct((sd, phys, rows, side), bf),
        in_specs=[hbm] * 6,
        out_specs=pl.BlockSpec(memory_space=pltpu.VMEM),
        scratch_shapes=[
            pltpu.SMEM(site_coeff.shape, jnp.float32),
            pltpu.SMEM(sub_sector.shape, jnp.int32),
            pltpu.SMEM(sub_sector.shape, jnp.int32),
            pltpu.SMEM(site_coeff.shape, jnp.float32),
            pltpu.VMEM(site_coeff.shape, jnp.float32),
            dma((4,)),
            pltpu.VMEM((sd, phys, side, side), bf),
            pltpu.VMEM((sd, nch, side, tc * side), bf),
            pltpu.VMEM((sd, side, tc * side), bf),
            pltpu.VMEM((sd * phys, side, side), jnp.float32),
            pltpu.VMEM((sd * phys, side // 2, side), jnp.float32),
            pltpu.VMEM((GROUPS, qg, half, rows, side), bf),
            pltpu.VMEM((GROUPS, qg, half, rows, side), bf),
        ]
        + [pltpu.VMEM((GROUPS, qg, rows, side), bf)] * 4
        + [pltpu.VMEM((n, tc, sd, side, side), bf)] * (nch - 1)
        + [pltpu.VMEM((n, 2, tc, sd, side // 2, side), bf)]
        + [pltpu.VMEM((sd * phys, tc * side, side), bf)] * (nch - 1)
        + [pltpu.VMEM((sd * phys, 2 * tc * side, side), bf)]
        + [dma, dma((nch,)), dma((nt, sd)), dma((nch, n)), dma((nch, n)), dma((nch, n))]
        + [dma((GROUPS,))] * 6
        + [dma((2 + tc * sd,))] * 2,
        compiler_params=pltpu.CompilerParams(
            collective_id=0, has_side_effects=True, vmem_limit_bytes=63 << 20
        ),
        cost_estimate=pl.CostEstimate(flops=flops, bytes_accessed=4 << 20, transcendentals=0),
        name="sigma",
    )(wave_blocks, right_env, left_env, site_coeff, dest_owner.reshape(sub_sector.shape), sub_sector)


def solution(mesh):
    placed = (
        P(("grp", "sec"), None, None, None),
        P(("grp", "term"), "sec", None, None),
        P(("grp", "term"), "sec", None, None),
        P(("grp", "term"), None),
        P("grp", None, None),
        P("grp", None),
    )
    return jax.shard_map(
        functools.partial(local, mesh.shape["sec"], mesh.shape["term"]),
        mesh=mesh,
        in_specs=placed,
        out_specs=P(("grp", "sec"), None, "term", None),
        check_vma=False,
    )
```

```python
import functools

import jax
import jax.numpy as jnp
from jax import lax
from jax.experimental import pallas as pl
from jax.experimental.pallas import tpu as pltpu
from jax.sharding import PartitionSpec as P

MESH = pl.DeviceIdType.MESH
GROUPS = 4


def body(
    n, nt, tc, sd, phys, side, nterm,
    wb_hbm, r_hbm, l_hbm, coeff_hbm, owner_hbm, sub_hbm, out_ref,
    coeff, owner_ref, sub_ref, coeff_x, coeff_v, small_sem, wb, rcat, rcat_x, acc, bacc, s1, r1, s2, r2, s3, r3, *rest,
):
    nch = nt // tc
    gath, wave = rest[:nch], rest[nch:2 * nch]
    load_sem, lsem, rl_sem, send_r, send_l, recv, ssem1, rsem1, ssem2, rsem2, ssem3, rsem3, xs, xr = rest[2 * nch:]
    last = nch - 1
    hr = side // 2
    g, i, t = lax.axis_index("grp"), lax.axis_index("sec"), lax.axis_index("term")
    q_all = sd * phys
    qg = q_all // GROUPS
    rows = side // nterm
    half = nterm // 2
    low = lax.rem(t, 2)
    high = t // 2
    pair = t + 1 - 2 * low
    across = lax.rem(t + half, nterm)
    has_r, has_l = i < n - 1, i > 0
    right, left = (g, jnp.minimum(i + 1, n - 1), t), (g, jnp.maximum(i - 1, 0), t)

    wb_load = pltpu.make_async_copy(wb_hbm, wb, load_sem)
    wb_load.start()
    small_loads = [
        pltpu.make_async_copy(src, dst, small_sem.at[k])
        for k, (src, dst) in enumerate(((coeff_hbm, coeff), (owner_hbm, owner_ref), (sub_hbm, sub_ref)))
    ]
    for cp in small_loads:
        cp.start()
    r_loads = []
    for k in range(nt):
        for r in range(sd):
            cp = pltpu.make_async_copy(
                r_hbm.at[k, r], rcat.at[r, k // tc, :, pl.ds((k % tc) * side, side)], rl_sem.at[k, r]
            )
            cp.start()
            r_loads.append(cp)
    own_loads = []
    for c in range(nch):
        if c == last:
            my_rows = pl.ds(pl.multiple_of(high * hr, hr), hr)
            cp = pltpu.make_async_copy(
                l_hbm.at[pl.ds(c * tc, tc), :, my_rows], gath[c].at[i, 0], lsem.at[c]
            )
        else:
            cp = pltpu.make_async_copy(l_hbm.at[pl.ds(c * tc, tc)], gath[c].at[i], lsem.at[c])
        cp.start()
        own_loads.append(cp)

    barrier = pltpu.get_barrier_semaphore()

    @pl.when(has_r)
    def _():
        pl.semaphore_signal(barrier, inc=1, device_id=right, device_id_type=MESH)

    @pl.when(has_l)
    def _():
        pl.semaphore_signal(barrier, inc=1, device_id=left, device_id_type=MESH)

    for peer in (pair, across):
        pl.semaphore_signal(barrier, inc=1, device_id=(g, i, peer), device_id_type=MESH)
    pl.semaphore_wait(barrier, 2 + has_r.astype(jnp.int32) + has_l.astype(jnp.int32))

    def piece(c, origin, to_right, own):
        dst = gath[c].at[origin]
        src = l_hbm.at[pl.ds(c * tc, tc)] if own and c != last else dst
        return pltpu.make_async_remote_copy(
            src_ref=src, dst_ref=dst,
            send_sem=(send_r if to_right else send_l).at[c, origin],
            recv_sem=recv.at[c, origin],
            device_id=right if to_right else left, device_id_type=MESH,
        )

    def send_own(c):
        @pl.when(has_r)
        def _():
            piece(c, i, True, True).start()

        @pl.when(has_l)
        def _():
            piece(c, i, False, True).start()

    send_own(0)

    def swap(k, src, dst):
        return pltpu.make_async_remote_copy(
            src_ref=src, dst_ref=dst, send_sem=xs.at[k], recv_sem=xr.at[k],
            device_id=(g, i, across), device_id_type=MESH,
        )

    their_rows = pl.ds(pl.multiple_of((1 - high) * hr, hr), hr)
    swap_l = swap(0, l_hbm.at[pl.ds(last * tc, tc), :, their_rows], gath[last].at[i, 1])
    swap_c = swap(1, coeff_hbm, coeff_v)
    swap_r = [
        swap(2 + u * sd + r, r_hbm.at[last * tc + u, r], rcat_x.at[r, :, pl.ds(u * side, side)])
        for u in range(tc) for r in range(sd)
    ]
    swaps = [swap_l, swap_c] + swap_r
    for cp in swaps:
        cp.start()
    for c in range(1, last):
        send_own(c)

    def relay(s, c):
        from_l, from_r = i - 1 - s, i + 1 + s

        @pl.when(from_l >= 0)
        def _():
            piece(c, from_l, True, False).wait_recv()

            @pl.when(has_r)
            def _():
                piece(c, from_l, True, False).start()

        @pl.when(from_r <= n - 1)
        def _():
            piece(c, from_r, False, False).wait_recv()

            @pl.when(has_l)
            def _():
                piece(c, from_r, False, False).start()

    wb_load.wait()
    for cp in small_loads:
        cp.wait()
    for cp in r_loads:
        cp.wait()

    def wave_part(r, lo, hi, theirs=False):
        def step(k, _):
            for c in (last,) if theirs else range(nch):
                s0 = 2 * k
                lhs = wb[r, pl.ds(s0, 2)].reshape(2 * side, side)
                rhs = rcat_x[r] if theirs else rcat[r, c]
                prod = jnp.dot(lhs, rhs, preferred_element_type=jnp.float32)
                for j in range(2):
                    for u in range(tc):
                        scale = (coeff_x if theirs else coeff)[c * tc + u, s0 + j]
                        scaled = prod[j * side:(j + 1) * side, u * side:(u + 1) * side] * scale
                        at = (u + (tc if theirs else 0)) * side
                        wave[c][r * phys + s0 + j, at:at + side, :] = scaled.astype(jnp.bfloat16)
            return 0

        lax.fori_loop(lo, hi, step, 0)

    def product(c, q):
        r, s = q // phys, lax.rem(q, phys)
        own, sub = owner_ref[i * sd + r, s], sub_ref[i * sd + r, s]
        if c == last:
            parts = [gath[c][own, h, u, sub] for h in range(2) for u in range(tc)]
        else:
            parts = [gath[c][own, u, sub] for u in range(tc)]
        lhs = jnp.concatenate(parts, axis=1)
        return jnp.dot(lhs, wave[c][q], preferred_element_type=jnp.float32)

    pairs = phys // 2
    wave_part(0, 0, pairs)
    if n > 2:
        relay(0, 0)
    for r in range(1, sd):
        wave_part(r, 0, pairs)
    if n > 2:
        for c in range(1, last):
            relay(0, c)
    for cp in swaps:
        cp.wait_recv()
    to_scalar = pltpu.make_async_copy(coeff_v, coeff_x, small_sem.at[3])
    to_scalar.start()
    to_scalar.wait()
    for r in range(sd):
        wave_part(r, 0, pairs, True)

    def steps(s, _):
        for c in range(last):
            relay(s, c)
        return 0

    if n > 3:
        lax.fori_loop(1, n - 2, steps, 0)
    for cp in own_loads:
        cp.wait()
    send_own(last)

    for c in range(last - 1):
        relay(n - 2, c)

        def add(q, _, c=c):
            p = product(c, q)
            acc[q] = p if c == 0 else acc[q] + p
            return 0

        lax.fori_loop(0, q_all, add, 0, unroll=4)
    relay(n - 2, last - 1)
    inner = jnp.logical_and(has_r, has_l)

    @pl.when(inner)
    def _():
        relay(0, last)

    def hop1(k):
        return pltpu.make_async_remote_copy(
            src_ref=s1.at[k], dst_ref=r1.at[k], send_sem=ssem1.at[k], recv_sem=rsem1.at[k],
            device_id=(g, i, pair), device_id_type=MESH,
        )

    def hop2(k):
        return pltpu.make_async_remote_copy(
            src_ref=s2.at[k], dst_ref=r2.at[k], send_sem=ssem2.at[k], recv_sem=rsem2.at[k],
            device_id=(g, i, across), device_id_type=MESH,
        )

    def hop3(k):
        return pltpu.make_async_remote_copy(
            src_ref=s3.at[k], dst_ref=r3.at[k], send_sem=ssem3.at[k], recv_sem=rsem3.at[k],
            device_id=(g, i, pair), device_id_type=MESH,
        )

    def rows_of(dest):
        return pl.ds(pl.multiple_of(dest * rows, rows), rows)

    def middle(k):
        hop1(k).wait_recv()

        def one(j, _):
            q = k * qg + j
            away = acc[q, rows_of((1 - high) * 2 + low)] + r1[k, j, 1 - high].astype(jnp.float32)
            s2[k, j] = away.astype(jnp.bfloat16)
            return 0

        lax.fori_loop(0, qg, one, 0, unroll=4)
        hop2(k).start()

    for k in range(GROUPS):
        def finish(j, _, k=k):
            q = k * qg + j
            p = product(last - 1, q)
            acc[q] = p if last == 1 else acc[q] + p
            for h in range(half):
                s1[k, j, h] = acc[q, rows_of(2 * h + 1 - low)].astype(jnp.bfloat16)
            return 0

        lax.fori_loop(0, qg, finish, 0, unroll=4)
        hop1(k).start()
        if k >= 1:
            middle(k - 1)
    middle(GROUPS - 1)

    def tail_steps(s, _):
        @pl.when(jnp.logical_not(jnp.logical_and(inner, s == 0)))
        def _():
            relay(s, last)

        return 0

    lax.fori_loop(0, n - 1, tail_steps, 0)
    for k in range(GROUPS):
        def tail(j, _, k=k):
            q = k * qg + j
            bacc[q] = product(last, q)
            s3[k, j] = bacc[q, rows_of(1 - low)].astype(jnp.bfloat16)
            return 0

        lax.fori_loop(0, qg, tail, 0, unroll=8)
        hop3(k).start()
    for k in range(GROUPS):
        hop2(k).wait_recv()
        hop3(k).wait_recv()

        def close(j, _, k=k):
            q = k * qg + j
            mine = acc[q, rows_of(t)] + r1[k, j, high].astype(jnp.float32)
            total = mine + r2[k, j].astype(jnp.float32)
            total = total + bacc[q, rows_of(low)] + r3[k, j].astype(jnp.float32)
            out_ref[q // phys, lax.rem(q, phys)] = total.astype(jnp.bfloat16)
            return 0

        lax.fori_loop(0, qg, close, 0, unroll=8)

    for k in range(GROUPS):
        hop1(k).wait_send()
        hop2(k).wait_send()
        hop3(k).wait_send()
    for cp in swaps:
        cp.wait_send()

    def drain(o, _):
        for c in range(nch):
            @pl.when(jnp.logical_and(has_r, o <= i))
            def _(c=c):
                piece(c, o, True, False).wait_send()

            @pl.when(jnp.logical_and(has_l, o >= i))
            def _(c=c):
                piece(c, o, False, False).wait_send()
        return 0

    lax.fori_loop(0, n, drain, 0)


def local(n, nterm, wave_blocks, right_env, left_env, site_coeff, dest_owner, sub_sector):
    sd, phys, side, _ = wave_blocks.shape
    nt = right_env.shape[0]
    tc = 2 if nt % 2 == 0 else 1
    nch = nt // tc
    rows, half, qg = side // nterm, nterm // 2, sd * phys // GROUPS
    bf, dma = jnp.bfloat16, pltpu.SemaphoreType.DMA
    hbm = pl.BlockSpec(memory_space=pltpu.HBM)
    flops = 4 * nt * sd * phys * side ** 3
    return pl.pallas_call(
        functools.partial(body, n, nt, tc, sd, phys, side, nterm),
        out_shape=jax.ShapeDtypeStruct((sd, phys, rows, side), bf),
        in_specs=[hbm] * 6,
        out_specs=pl.BlockSpec(memory_space=pltpu.VMEM),
        scratch_shapes=[
            pltpu.SMEM(site_coeff.shape, jnp.float32),
            pltpu.SMEM(sub_sector.shape, jnp.int32),
            pltpu.SMEM(sub_sector.shape, jnp.int32),
            pltpu.SMEM(site_coeff.shape, jnp.float32),
            pltpu.VMEM(site_coeff.shape, jnp.float32),
            dma((4,)),
            pltpu.VMEM((sd, phys, side, side), bf),
            pltpu.VMEM((sd, nch, side, tc * side), bf),
            pltpu.VMEM((sd, side, tc * side), bf),
            pltpu.VMEM((sd * phys, side, side), jnp.float32),
            pltpu.VMEM((sd * phys, side // 2, side), jnp.float32),
            pltpu.VMEM((GROUPS, qg, half, rows, side), bf),
            pltpu.VMEM((GROUPS, qg, half, rows, side), bf),
        ]
        + [pltpu.VMEM((GROUPS, qg, rows, side), bf)] * 4
        + [pltpu.VMEM((n, tc, sd, side, side), bf)] * (nch - 1)
        + [pltpu.VMEM((n, 2, tc, sd, side // 2, side), bf)]
        + [pltpu.VMEM((sd * phys, tc * side, side), bf)] * (nch - 1)
        + [pltpu.VMEM((sd * phys, 2 * tc * side, side), bf)]
        + [dma, dma((nch,)), dma((nt, sd)), dma((nch, n)), dma((nch, n)), dma((nch, n))]
        + [dma((GROUPS,))] * 6
        + [dma((2 + tc * sd,))] * 2,
        compiler_params=pltpu.CompilerParams(
            collective_id=0, has_side_effects=True, vmem_limit_bytes=63 << 20
        ),
        cost_estimate=pl.CostEstimate(flops=flops, bytes_accessed=4 << 20, transcendentals=0),
        name="sigma",
    )(wave_blocks, right_env, left_env, site_coeff, dest_owner.reshape(sub_sector.shape), sub_sector)


def solution(mesh):
    placed = (
        P(("grp", "sec"), None, None, None),
        P(("grp", "term"), "sec", None, None),
        P(("grp", "term"), "sec", None, None),
        P(("grp", "term"), None),
        P("grp", None, None),
        P("grp", None),
    )
    return jax.shard_map(
        functools.partial(local, mesh.shape["sec"], mesh.shape["term"]),
        mesh=mesh,
        in_specs=placed,
        out_specs=P(("grp", "sec"), None, "term", None),
        check_vma=False,
    )
```
